512 devices in a mesh: band: 8 (over x, core), sub: 64 (over z, y).
Axes of the slice: x: 4, y: 4, z: 16, core: 2. Of those that a mesh axis runs over, the one named last changes fastest.
Arguments:
- spectra: bfloat16 [64, 64, 128, 256], P('sub', None, 'band'), parts along dimension 2, may hold values from -500 to 500
- bin_freqs: float32 [128], P('band'), parts along dimension 0, may hold values from 0.5 to 5
- station_offsets: float32 [2, 128], replicated, may hold values from -1 to 1
- beam_grid: int32 [64], replicated, may hold values from 0 to 255, as said below
- owner_subarrays: int32 [64, 4], replicated, may hold values from 0 to 63, as said below
- pair_slots: int32 [64, 6, 2], P('sub'), may hold values from 0 to 3, as said below
- pair_count: int32 [64], P('sub'), may hold values from 1 to 6, as said below
Outputs:
- power: float32 [384, 512, 64], P('sub', 'band'), parts along dimension 1
The draws below stay inside these ranges and needn't reach their ends.
There are 8 independent parts, one for each index of `band`. The reference program is written for one: setup_inputs(seed, part) draws one part's arguments, and reference() takes and returns one part's arrays. A program takes and returns all parts, laid end to end along the dimension named above; an argument that names none is the same for every part. Nothing has to cross between parts.
Inputs may be any that keep to these rules, and one draw needn't show every extreme that they name: `beam_grid`: within each part 64 distinct nodes; nodes 0 and 255 are always among them. `owner_subarrays`: each owner's row holds 4 distinct subarrays; every subarray is held by some owner. `pair_slots`: each owner's slots name distinct unordered pairs of two different positions, first below second. `pair_count`: one owner has all 6 slots live.
All inputs are finite; a program needn't handle non-finite values.
Results may differ from the reference program's by a relative error of at most 0.0026.
Values may be sent and summed in bfloat16 or wider, within the bound.
No kernel may reach another device: no remote copies, remote signals or barrier semaphores. Data moves between devices by JAX's collectives and lax.ppermute only.
A program may use at most 64 MiB of HBM per device.

```python
import math
import jax
import jax.numpy as jnp
import numpy as np
from jax import lax

STATIONS = 128
BEAMS = 64
SUBARRAYS = 64
BINS = 16
GRID = 256
NEED = 4
PAIR_CAP = 6
RECORDS = 64
OWNERS = 64


def draw_spectra(key, part):
    key = jax.random.fold_in(key, 11)
    first_key, second_key, third_key = jax.random.split(key, 3)
    shape = (RECORDS, SUBARRAYS, BINS, 2 * STATIONS)
    base = jnp.clip(jax.random.normal(first_key, shape, jnp.float32), -6.0, 6.0)
    rise = 3.0
    top = 10.0
    position = jnp.arange(RECORDS, dtype=jnp.float32) / max(RECORDS - 1, 1)
    record_scale = jnp.exp(math.log(rise) * position)
    station_scale = jnp.exp(jax.random.uniform(second_key, (SUBARRAYS, 1, STATIONS), jnp.float32, 0.0, math.log(top)))
    station_scale = jnp.concatenate([station_scale, station_scale], axis=2)
    rough = jnp.exp(jax.random.uniform(third_key, shape, jnp.float32, -0.7, 0.7))
    return (base * rough * record_scale[:, None, None, None] * station_scale[None]).astype(jnp.bfloat16)


def draw_beam_grid(key, part):
    key = jax.random.fold_in(key, 12)
    first_key, second_key = jax.random.split(key)
    inner = jax.random.permutation(first_key, GRID - 2) + 1
    chosen = jnp.concatenate([jnp.array([0, GRID - 1], jnp.int32), inner[:BEAMS - 2].astype(jnp.int32)])
    order = jax.random.permutation(second_key, BEAMS)
    return chosen[order].astype(jnp.int32)


def draw_owner_subarrays(key, part):
    key = jax.random.fold_in(key, 13)
    base = jax.random.permutation(key, SUBARRAYS).astype(jnp.int32)
    index = (jnp.arange(OWNERS, dtype=jnp.int32)[:, None] * NEED + jnp.arange(NEED, dtype=jnp.int32)[None, :]) % SUBARRAYS
    return base[index]


def draw_pair_slots(key, part):
    key = jax.random.fold_in(key, 14)
    rows, cols = np.triu_indices(NEED, 1)
    table = jnp.asarray(np.stack([rows, cols], axis=-1).astype(np.int32))
    keys = jax.random.split(key, OWNERS)
    orders = jax.vmap(lambda single: jax.random.permutation(single, table.shape[0]))(keys)[:, :PAIR_CAP]
    return table[orders].astype(jnp.int32)


def draw_pair_count(key, part):
    key = jax.random.fold_in(key, 15)
    first_key, second_key = jax.random.split(key)
    counts = jax.random.randint(first_key, (OWNERS,), 1, 3, jnp.int32)
    busiest = jax.random.randint(second_key, (), 0, OWNERS, jnp.int32)
    return counts.at[busiest].set(PAIR_CAP).astype(jnp.int32)


def setup_inputs(seed: int = 0, part: int = 0) -> dict:
    seeds = jax.random.split(jax.random.key(seed), 8)
    part_keys = jax.random.split(jax.random.fold_in(seeds[7], part), 8)
    spectra = draw_spectra(jax.random.fold_in(jax.random.fold_in(seeds[7], part), 71), part)
    bin_freqs = jnp.clip(jax.random.uniform(part_keys[1], (BINS,), jnp.float32, 0.5, 5.0), 0.5, 5.0)
    station_offsets = jnp.clip(jax.random.uniform(seeds[2], (2, STATIONS), jnp.float32, -1.0, 1.0), -1.0, 1.0)
    beam_grid = draw_beam_grid(jax.random.fold_in(seeds[7], 71), part)
    owner_subarrays = draw_owner_subarrays(jax.random.fold_in(seeds[7], 71), part)
    pair_slots = draw_pair_slots(jax.random.fold_in(seeds[7], 71), part)
    pair_count = draw_pair_count(jax.random.fold_in(seeds[7], 71), part)
    return {"spectra": spectra, "bin_freqs": bin_freqs, "station_offsets": station_offsets, "beam_grid": beam_grid, "owner_subarrays": owner_subarrays, "pair_slots": pair_slots, "pair_count": pair_count}


slow_step = 0.04
eps = 1e-06

def steering(bin_freqs, station_offsets, beam_grid):
    slow_x = ((beam_grid % 16).astype(jnp.float32) - 7.5) * slow_step
    slow_y = ((beam_grid // 16).astype(jnp.float32) - 7.5) * slow_step
    delay = slow_x[:, None] * station_offsets[0][None, :] + slow_y[:, None] * station_offsets[1][None, :]
    phase = 2.0 * math.pi * bin_freqs[:, None, None] * delay[None, :, :]
    factor = station_offsets.shape[1] ** (-0.5)
    cosine = jnp.swapaxes(jnp.cos(phase), 1, 2) * factor
    sine = jnp.swapaxes(jnp.sin(phase), 1, 2) * factor
    upper = jnp.concatenate([cosine, -sine], axis=2)
    lower = jnp.concatenate([sine, cosine], axis=2)
    return jnp.concatenate([upper, lower], axis=1).astype(jnp.bfloat16)

def reference(spectra, bin_freqs, station_offsets, beam_grid, owner_subarrays, pair_slots, pair_count):
    values = spectra.astype(jnp.float32)
    half = values.shape[-1] // 2
    energy = lax.optimization_barrier(jnp.sum(values * values, axis=(0, 2)))
    energy = energy[:, :half] + energy[:, half:]
    scale = lax.rsqrt(energy / (RECORDS * BINS) + eps)
    scale = jnp.concatenate([scale, scale], axis=1)
    whitened = (values * scale[None, :, None, :]).astype(jnp.bfloat16)
    matrix = steering(bin_freqs, station_offsets, beam_grid)
    beams = jnp.einsum('rqns,nsb->rqnb', whitened.astype(jnp.float32), matrix.astype(jnp.float32)).astype(jnp.bfloat16)

    def owner_power(operands):
        held_ids, slots, count = operands
        held = beams[:, held_ids]

        def slot_power(pair):
            first = held[:, pair[0]].astype(jnp.float32)
            second = held[:, pair[1]].astype(jnp.float32)
            product = jnp.einsum('rnb,rnc->nbc', first, second)
            real = product[:, :BEAMS, :BEAMS] + product[:, BEAMS:, BEAMS:]
            imag = product[:, BEAMS:, :BEAMS] - product[:, :BEAMS, BEAMS:]
            return lax.optimization_barrier(jnp.sum(real * real + imag * imag, axis=0)) / (BINS * RECORDS)
        powers = lax.map(slot_power, slots)
        live = jnp.arange(PAIR_CAP, dtype=jnp.int32) < count
        return jnp.where(live[:, None, None], powers, jnp.zeros_like(powers))
    power = lax.map(owner_power, (owner_subarrays, pair_slots, pair_count))
    return power.reshape(OWNERS * PAIR_CAP, BEAMS, BEAMS)
```

```python
import math

import jax
import jax.numpy as jnp
from jax import lax
from jax.sharding import Mesh
from jax.sharding import PartitionSpec as P

ROWS = 4
SUB = ("z", "y")

slow_step = 0.04
eps = 1e-06


def steering(bin_freqs, station_offsets, beam_grid):
    slow_x = ((beam_grid % 16).astype(jnp.float32) - 7.5) * slow_step
    slow_y = ((beam_grid // 16).astype(jnp.float32) - 7.5) * slow_step
    delay = (
        slow_x[:, None] * station_offsets[0][None, :]
        + slow_y[:, None] * station_offsets[1][None, :]
    )
    phase = 2.0 * math.pi * bin_freqs[:, None, None] * delay[None, :, :]
    factor = station_offsets.shape[1] ** (-0.5)
    cosine = jnp.swapaxes(jnp.cos(phase), 1, 2) * factor
    sine = jnp.swapaxes(jnp.sin(phase), 1, 2) * factor
    upper = jnp.concatenate([cosine, -sine], axis=2)
    lower = jnp.concatenate([sine, cosine], axis=2)
    return jnp.concatenate([upper, lower], axis=1).astype(jnp.bfloat16)


def spread(block, size, axis):
    copies = jnp.broadcast_to(block[None], (size, *block.shape))
    return lax.all_to_all(copies, axis, 0, 0, tiled=True)


def sum_over_sub(energy):
    depth, rows = lax.axis_size("z"), lax.axis_size("y")
    parts = energy.reshape(rows, -1, energy.shape[1])
    group = jnp.sum(lax.all_to_all(parts, "y", 0, 0, tiled=True), axis=0)
    group = jnp.sum(spread(group, depth, "z"), axis=0)
    return spread(group, rows, "y").reshape(energy.shape)


def pair_power(held, pair, divisor):
    first = lax.dynamic_index_in_dim(held, pair[0], 1, keepdims=False)
    second = lax.dynamic_index_in_dim(held, pair[1], 1, keepdims=False)
    product = jnp.einsum("rnb,rnc->nbc", first, second, preferred_element_type=jnp.float32)
    half = product.shape[-1] // 2
    real = product[:, :half, :half] + product[:, half:, half:]
    imag = product[:, half:, :half] - product[:, :half, half:]
    return jnp.sum(real * real + imag * imag, axis=0) / divisor


def shards(spectra, bin_freqs, station_offsets, beam_grid, owner_subarrays, pair_slots, pair_count):
    local_records = spectra.shape[0]
    records = (lax.axis_size("z") * lax.axis_size("y")) * local_records
    bins = spectra.shape[2]
    stations = spectra.shape[3] // 2
    owners = owner_subarrays.shape[0]
    held_count = owner_subarrays.shape[1]
    energy = jnp.sum(jnp.square(spectra.astype(jnp.float32)), axis=(0, 2))
    energy = energy[:, :stations] + energy[:, stations:]
    energy = sum_over_sub(energy)
    scale = lax.rsqrt(energy / (records * bins) + eps)
    scale = jnp.concatenate([scale, scale], axis=1)
    whitened = (spectra.astype(jnp.float32) * scale[None, :, None, :]).astype(jnp.bfloat16)
    matrix = steering(bin_freqs, station_offsets, beam_grid)
    flat_ids = owner_subarrays.reshape(-1)
    beams = jnp.einsum(
        "rqns,nsb->rqnb", whitened, matrix, preferred_element_type=jnp.float32
    ).astype(jnp.bfloat16)
    outgoing = jnp.take(beams, flat_ids, axis=1)
    outgoing = outgoing.reshape(local_records, owners, held_count, bins, beams.shape[-1])
    held = lax.all_to_all(outgoing, SUB, split_axis=1, concat_axis=0, tiled=True)
    held = held.reshape(records, held_count, bins, held.shape[-1])
    slots = pair_slots[0]
    count = pair_count[0]
    half = held.shape[-1] // 2
    divisor = bins * records
    empty = jnp.zeros((slots.shape[0], half, half), jnp.float32)

    def add_slot(index, total):
        return lax.dynamic_update_index_in_dim(
            total, pair_power(held, slots[index], divisor), index, 0
        )

    power = lax.fori_loop(0, count, add_slot, empty)
    return power


def solution(mesh):
    bands, subs = mesh.devices.shape
    grid = Mesh(mesh.devices.reshape(bands, subs // ROWS, ROWS), ("band", "z", "y"))
    return jax.shard_map(
        shards,
        mesh=grid,
        in_specs=(
            P(SUB, None, "band", None),
            P("band"),
            P(),
            P(),
            P(),
            P(SUB, None, None),
            P(SUB),
        ),
        out_specs=P(SUB, "band", None),
        check_vma=False,
    )
```

```python
import functools
import math

import jax
import jax.numpy as jnp
from jax import lax
from jax.experimental import pallas as pl
from jax.experimental.pallas import tpu as pltpu
from jax.sharding import Mesh
from jax.sharding import PartitionSpec as P

ROWS = 4
SUB = ("z", "y")

slow_step = 0.04
eps = 1e-06


def steering(bin_freqs, station_offsets, beam_grid):
    slow_x = ((beam_grid % 16).astype(jnp.float32) - 7.5) * slow_step
    slow_y = ((beam_grid // 16).astype(jnp.float32) - 7.5) * slow_step
    delay = (
        slow_x[:, None] * station_offsets[0][None, :]
        + slow_y[:, None] * station_offsets[1][None, :]
    )
    phase = 2.0 * math.pi * bin_freqs[:, None, None] * delay[None, :, :]
    factor = station_offsets.shape[1] ** (-0.5)
    cosine = jnp.swapaxes(jnp.cos(phase), 1, 2) * factor
    sine = jnp.swapaxes(jnp.sin(phase), 1, 2) * factor
    upper = jnp.concatenate([cosine, -sine], axis=2)
    lower = jnp.concatenate([sine, cosine], axis=2)
    return jnp.concatenate([upper, lower], axis=1).astype(jnp.bfloat16)


def spread(block, size, axis):
    copies = jnp.broadcast_to(block[None], (size, *block.shape))
    return lax.all_to_all(copies, axis, 0, 0, tiled=True)


def sum_over_sub(energy):
    depth, rows = lax.axis_size("z"), lax.axis_size("y")
    parts = energy.reshape(rows, -1, energy.shape[1])
    group = jnp.sum(lax.all_to_all(parts, "y", 0, 0, tiled=True), axis=0)
    group = jnp.sum(spread(group, depth, "z"), axis=0)
    return spread(group, rows, "y").reshape(energy.shape)


def pair_kernel(bins, slots_ref, count_ref, held_ref, power_ref, wide, most, rest, picked):
    records, rows, width = held_ref.shape
    half = width // 2
    wide[...] = held_ref[...].astype(jnp.float32).reshape(wide.shape)
    low = lax.broadcasted_iota(jnp.int32, (records, width), 1) < half
    most[...] = jnp.zeros_like(most)
    rest[...] = jnp.zeros_like(rest)
    for n in range(bins):
        held = [wide[pl.ds(h * bins + n, records, stride=rows), :] for h in range(4)]
        turned = [pltpu.roll(x, half, 1) for x in held]
        real = jnp.concatenate([jnp.where(low, held[0], turned[1]), held[2]], axis=1)
        imag = jnp.concatenate([jnp.where(low, turned[0], held[1]), turned[2]], axis=1)
        first = jnp.concatenate([real, imag], axis=0)[:, : 3 * half].astype(jnp.bfloat16)
        second = [
            jnp.concatenate([jnp.where(low, held[h], -held[h]), turned[h]], axis=0)
            for h in range(1, 4)
        ]
        one = second[0].astype(jnp.bfloat16)
        two = jnp.concatenate(second[1:], axis=1).astype(jnp.bfloat16)
        dims = (((0,), (0,)), ((), ()))
        cross = lax.dot_general(first, two, dims, preferred_element_type=jnp.float32)
        most[...] += cross * cross
        cross = lax.dot_general(first[:, :half], one, dims, preferred_element_type=jnp.float32)
        rest[...] += cross * cross
    picked[0, :half] = rest[:, :half] + rest[:, half:]
    picked[1] = most[:, :half] + most[:, half:width]
    picked[2] = most[:, width : width + half] + most[:, width + half :]
    for p in range(power_ref.shape[0]):
        row = pl.multiple_of(slots_ref[p, 0] * half, half)
        power = picked[slots_ref[p, 1] - 1, pl.ds(row, half), :] / (bins * records)
        power_ref[p] = jnp.where(p < count_ref[0], power, 0.0)


def pair_powers(slots, count, held, bins):
    records, rows, width = held.shape
    half = width // 2
    return pl.pallas_call(
        functools.partial(pair_kernel, bins),
        out_shape=jax.ShapeDtypeStruct((slots.shape[0], half, half), jnp.float32),
        in_specs=[
            pl.BlockSpec(memory_space=pltpu.SMEM),
            pl.BlockSpec(memory_space=pltpu.SMEM),
            pl.BlockSpec(memory_space=pltpu.VMEM),
        ],
        out_specs=pl.BlockSpec(memory_space=pltpu.VMEM),
        scratch_shapes=[
            pltpu.VMEM((records * rows, width), jnp.float32),
            pltpu.VMEM((3 * half, 2 * width), jnp.float32),
            pltpu.VMEM((half, width), jnp.float32),
            pltpu.VMEM((3, 3 * half, half), jnp.float32),
        ],
        compiler_params=pltpu.CompilerParams(vmem_limit_bytes=32 * 1024 * 1024),
        cost_estimate=pl.CostEstimate(
            flops=2 * bins * 2 * records * 4 * half * 6 * half,
            bytes_accessed=held.size * 2,
            transcendentals=0,
        ),
    )(slots, count, held)


def shards(spectra, bin_freqs, station_offsets, beam_grid, owner_subarrays, pair_slots, pair_count):
    local_records = spectra.shape[0]
    records = (lax.axis_size("z") * lax.axis_size("y")) * local_records
    bins = spectra.shape[2]
    stations = spectra.shape[3] // 2
    owners = owner_subarrays.shape[0]
    held_count = owner_subarrays.shape[1]
    energy = jnp.sum(jnp.square(spectra.astype(jnp.float32)), axis=(0, 2))
    energy = energy[:, :stations] + energy[:, stations:]
    energy = sum_over_sub(energy)
    scale = lax.rsqrt(energy / (records * bins) + eps)
    scale = jnp.concatenate([scale, scale], axis=1)
    whitened = (spectra.astype(jnp.float32) * scale[None, :, None, :]).astype(jnp.bfloat16)
    matrix = steering(bin_freqs, station_offsets, beam_grid)
    flat_ids = owner_subarrays.reshape(-1)
    beams = jnp.einsum(
        "rqns,nsb->rqnb", whitened, matrix, preferred_element_type=jnp.float32
    ).astype(jnp.bfloat16)
    outgoing = beams.at[:, flat_ids].get(mode="promise_in_bounds")
    outgoing = outgoing.reshape(local_records, owners, held_count * bins, beams.shape[-1])
    held = lax.all_to_all(outgoing, SUB, split_axis=1, concat_axis=0, tiled=True)
    held = held.reshape(records, held_count * bins, held.shape[-1])
    return pair_powers(pair_slots[0], pair_count, held, bins)


def solution(mesh):
    bands, subs = mesh.devices.shape
    grid = Mesh(mesh.devices.reshape(bands, subs // ROWS, ROWS), ("band", "z", "y"))
    return jax.shard_map(
        shards,
        mesh=grid,
        in_specs=(
            P(SUB, None, "band", None),
            P("band"),
            P(),
            P(),
            P(),
            P(SUB, None, None),
            P(SUB),
        ),
        out_specs=P(SUB, "band", None),
        check_vma=False,
    )
```

```python
import functools
import math

import jax
import jax.numpy as jnp
from jax import lax
from jax.experimental import pallas as pl
from jax.experimental.pallas import tpu as pltpu
from jax.sharding import Mesh
from jax.sharding import PartitionSpec as P

ROWS = 4
ZL = 2
SUB = ("zh", "zl", "y")

slow_step = 0.04
eps = 1e-06


def steering(bin_freqs, station_offsets, beam_grid):
    slow_x = ((beam_grid % 16).astype(jnp.float32) - 7.5) * slow_step
    slow_y = ((beam_grid // 16).astype(jnp.float32) - 7.5) * slow_step
    delay = (
        slow_x[:, None] * station_offsets[0][None, :]
        + slow_y[:, None] * station_offsets[1][None, :]
    )
    phase = 2.0 * math.pi * bin_freqs[:, None, None] * delay[None, :, :]
    factor = station_offsets.shape[1] ** (-0.5)
    cosine = jnp.swapaxes(jnp.cos(phase), 1, 2) * factor
    sine = jnp.swapaxes(jnp.sin(phase), 1, 2) * factor
    upper = jnp.concatenate([cosine, -sine], axis=2)
    lower = jnp.concatenate([sine, cosine], axis=2)
    return jnp.concatenate([upper, lower], axis=1).astype(jnp.bfloat16)


def spread(block, size, axis):
    copies = jnp.broadcast_to(block[None], (size, *block.shape))
    return lax.all_to_all(copies, axis, 0, 0, tiled=True)


def sum_over_sub(energy):
    near = ("zl", "y")
    size = lax.axis_size(near)
    parts = energy.reshape(size, -1, energy.shape[1])
    group = jnp.sum(lax.all_to_all(parts, near, 0, 0, tiled=True), axis=0).astype(jnp.bfloat16)
    all_groups = spread(group, lax.axis_size(SUB), SUB).astype(jnp.float32)
    return jnp.sum(all_groups.reshape(-1, *energy.shape), axis=0)


def pair_kernel(bins, slots_ref, count_ref, held_ref, power_ref, turned_ref, most, rest, picked):
    records, _, width = held_ref.shape
    half = width // 2
    for h in range(4):
        turned_ref[h] = jnp.swapaxes(held_ref[:, h * bins : (h + 1) * bins, :], 0, 1)
    low = lax.broadcasted_iota(jnp.int32, (records, width), 1) < half
    most[...] = jnp.zeros_like(most)
    rest[...] = jnp.zeros_like(rest)
    for n in range(bins):
        held = [turned_ref[h, n] for h in range(4)]
        rolled = [pltpu.roll(x, half, 1) for x in held]
        real = jnp.concatenate([jnp.where(low, held[0], rolled[1]), held[2]], axis=1)
        imag = jnp.concatenate([jnp.where(low, rolled[0], held[1]), rolled[2]], axis=1)
        first = jnp.concatenate([real, imag], axis=0)[:, : 3 * half]
        second = [
            jnp.concatenate([jnp.where(low, held[h], -held[h]), rolled[h]], axis=0)
            for h in range(1, 4)
        ]
        two = jnp.concatenate(second[1:], axis=1)
        dims = (((0,), (0,)), ((), ()))
        cross = lax.dot_general(first, two, dims, preferred_element_type=jnp.float32)
        most[...] += cross * cross
        cross = lax.dot_general(
            first[:, :half], second[0], dims, preferred_element_type=jnp.float32
        )
        rest[...] += cross * cross
    picked[0, :half] = rest[:, :half] + rest[:, half:]
    picked[1] = most[:, :half] + most[:, half:width]
    picked[2] = most[:, width : width + half] + most[:, width + half :]
    for p in range(power_ref.shape[0]):
        row = pl.multiple_of(slots_ref[p, 0] * half, half)
        power = picked[slots_ref[p, 1] - 1, pl.ds(row, half), :] / (bins * records)
        power_ref[p] = jnp.where(p < count_ref[0], power, 0.0)


def pair_powers(slots, count, held, bins):
    records, rows, width = held.shape
    half = width // 2
    return pl.pallas_call(
        functools.partial(pair_kernel, bins),
        out_shape=jax.ShapeDtypeStruct((slots.shape[0], half, half), jnp.float32),
        in_specs=[
            pl.BlockSpec(memory_space=pltpu.SMEM),
            pl.BlockSpec(memory_space=pltpu.SMEM),
            pl.BlockSpec(memory_space=pltpu.VMEM),
        ],
        out_specs=pl.BlockSpec(memory_space=pltpu.VMEM),
        scratch_shapes=[
            pltpu.VMEM((4, bins, records, width), jnp.bfloat16),
            pltpu.VMEM((3 * half, 2 * width), jnp.float32),
            pltpu.VMEM((half, width), jnp.float32),
            pltpu.VMEM((3, 3 * half, half), jnp.float32),
        ],
        compiler_params=pltpu.CompilerParams(vmem_limit_bytes=32 * 1024 * 1024),
        cost_estimate=pl.CostEstimate(
            flops=2 * bins * 2 * records * 4 * half * 6 * half,
            bytes_accessed=held.size * 2,
            transcendentals=0,
        ),
    )(slots, count, held)


def shards(spectra, bin_freqs, station_offsets, beam_grid, owner_subarrays, pair_slots, pair_count):
    local_records = spectra.shape[0]
    records = lax.axis_size(SUB) * local_records
    bins = spectra.shape[2]
    stations = spectra.shape[3] // 2
    owners = owner_subarrays.shape[0]
    held_count = owner_subarrays.shape[1]
    energy = jnp.sum(jnp.square(spectra.astype(jnp.float32)), axis=(0, 2))
    energy = energy[:, :stations] + energy[:, stations:]
    energy = sum_over_sub(energy)
    scale = lax.rsqrt(energy / (records * bins) + eps)
    scale = jnp.concatenate([scale, scale], axis=1)
    whitened = (spectra.astype(jnp.float32) * scale[None, :, None, :]).astype(jnp.bfloat16)
    matrix = steering(bin_freqs, station_offsets, beam_grid)
    flat_ids = owner_subarrays.reshape(-1)
    beams = jnp.einsum(
        "rqns,nsb->rqnb", whitened, matrix, preferred_element_type=jnp.float32
    ).astype(jnp.bfloat16)
    outgoing = beams.at[:, flat_ids].get(mode="promise_in_bounds")
    outgoing = outgoing.reshape(local_records, owners, held_count * bins, beams.shape[-1])
    held = lax.all_to_all(outgoing, SUB, split_axis=1, concat_axis=0, tiled=True)
    held = held.reshape(records, held_count * bins, held.shape[-1])
    return pair_powers(pair_slots[0], pair_count, held, bins)


def solution(mesh):
    bands, subs = mesh.devices.shape
    grid = Mesh(mesh.devices.reshape(bands, subs // ROWS // ZL, ZL, ROWS), ("band", "zh", "zl", "y"))
    return jax.shard_map(
        shards,
        mesh=grid,
        in_specs=(
            P(SUB, None, "band", None),
            P("band"),
            P(),
            P(),
            P(),
            P(SUB, None, None),
            P(SUB),
        ),
        out_specs=P(SUB, "band", None),
        check_vma=False,
    )
```

```python
import functools
import math

import jax
import jax.numpy as jnp
import numpy as np
from jax import lax
from jax.experimental import pallas as pl
from jax.experimental.pallas import tpu as pltpu
from jax.sharding import PartitionSpec as P

COLUMNS = 4
NEAR = 8
FIRST = (8, 2)

slow_step = 0.04
eps = 1e-06


def steering(bin_freqs, station_offsets, beam_grid):
    slow_x = ((beam_grid % 16).astype(jnp.float32) - 7.5) * slow_step
    slow_y = ((beam_grid // 16).astype(jnp.float32) - 7.5) * slow_step
    delay = (
        slow_x[:, None] * station_offsets[0][None, :]
        + slow_y[:, None] * station_offsets[1][None, :]
    )
    phase = 2.0 * math.pi * bin_freqs[:, None, None] * delay[None, :, :]
    factor = station_offsets.shape[1] ** (-0.5)
    cosine = jnp.swapaxes(jnp.cos(phase), 1, 2) * factor
    sine = jnp.swapaxes(jnp.sin(phase), 1, 2) * factor
    upper = jnp.concatenate([cosine, -sine], axis=2)
    lower = jnp.concatenate([sine, cosine], axis=2)
    return jnp.concatenate([upper, lower], axis=1).astype(jnp.bfloat16)


def energy_parts(spectra, near):
    subarrays, _, width = spectra.shape
    values = spectra.astype(jnp.float32)
    real, imag = values[:, :, : width // 2], values[:, :, width // 2 :]
    energy = jnp.sum(real * real + imag * imag, axis=1)
    return energy.reshape(near, subarrays // near, width // 2)


def encode(energy):
    scaled = jnp.square(energy * (1.0 / 256.0))
    return jnp.square(scaled).astype(jnp.bfloat16)


def decode(code):
    return jnp.sqrt(jnp.sqrt(code.astype(jnp.float32))) * 256.0


def beam_kernel(count, ids_ref, code_ref, spectra_ref, matrix_ref, out_ref, made, turned, chunk, sems):
    bins, subarrays, width = spectra_ref.shape
    held = ids_ref.shape[1]
    steps, per_step = chunk.shape[0], chunk.shape[1]
    groups = decode(code_ref[...]).reshape(-1, subarrays, width // 2)
    scale = lax.rsqrt(jnp.sum(groups, axis=0) / count + eps)
    scale = jnp.concatenate([scale, scale], axis=1)
    for n in range(bins):
        white = (spectra_ref[n].astype(jnp.float32) * scale).astype(jnp.bfloat16)
        made[n] = jnp.dot(
            white, matrix_ref[n], preferred_element_type=jnp.float32
        ).astype(jnp.bfloat16)
    turned[...] = jnp.swapaxes(made[...], 0, 1)
    copies = []
    for step in range(steps):
        for own in range(per_step):
            for h in range(held):
                chunk[step, own, h * bins : (h + 1) * bins] = turned[
                    ids_ref[step * per_step + own, h]
                ]
        copies.append(
            pltpu.make_async_copy(
                chunk.at[step], out_ref.at[pl.ds(step * per_step, per_step)], sems.at[step]
            )
        )
        copies[-1].start()
    for copy in copies:
        copy.wait()


def outgoing_beams(ids, code, spectra, matrix, count):
    bins, subarrays, width = spectra.shape
    owners, held = ids.shape
    beams = matrix.shape[2]
    steps = 8
    smem = pl.BlockSpec(memory_space=pltpu.SMEM)
    vmem = pl.BlockSpec(memory_space=pltpu.VMEM)
    return pl.pallas_call(
        functools.partial(beam_kernel, count),
        out_shape=jax.ShapeDtypeStruct((owners, held * bins, beams), jnp.bfloat16),
        in_specs=[smem, vmem, vmem, vmem],
        out_specs=pl.BlockSpec(memory_space=pl.ANY),
        scratch_shapes=[
            pltpu.VMEM((bins, subarrays, beams), jnp.bfloat16),
            pltpu.VMEM((subarrays, bins, beams), jnp.bfloat16),
            pltpu.VMEM((steps, owners // steps, held * bins, beams), jnp.bfloat16),
            pltpu.SemaphoreType.DMA((steps,)),
        ],
        compiler_params=pltpu.CompilerParams(vmem_limit_bytes=32 * 1024 * 1024),
        cost_estimate=pl.CostEstimate(
            flops=2 * bins * subarrays * width * beams,
            bytes_accessed=2 * (spectra.size + owners * held * bins * beams),
            transcendentals=0,
        ),
    )(ids, code, spectra, matrix)


def pair_kernel(bins, slots_ref, count_ref, held_ref, power_ref, turned_ref, most, rest, picked, made, sems):
    records, _, width = held_ref.shape
    half = width // 2
    for h in range(4):
        turned_ref[h] = jnp.swapaxes(held_ref[:, h * bins : (h + 1) * bins, :], 0, 1)
    low = lax.broadcasted_iota(jnp.int32, (records, width), 1) < half
    most[...] = jnp.zeros_like(most)
    rest[...] = jnp.zeros_like(rest)
    for n in range(bins):
        held = [turned_ref[h, n] for h in range(4)]
        rolled = [pltpu.roll(x, half, 1) for x in held]
        real = jnp.concatenate([jnp.where(low, held[0], rolled[1]), held[2]], axis=1)
        imag = jnp.concatenate([jnp.where(low, rolled[0], held[1]), rolled[2]], axis=1)
        first = jnp.concatenate([real, imag], axis=0)[:, : 3 * half]
        second = [
            jnp.concatenate([jnp.where(low, held[h], -held[h]), rolled[h]], axis=0)
            for h in range(1, 4)
        ]
        two = jnp.concatenate(second[1:], axis=1)
        dims = (((0,), (0,)), ((), ()))
        cross = lax.dot_general(first, two, dims, preferred_element_type=jnp.float32)
        most[...] += cross * cross
        cross = lax.dot_general(
            first[:, :half], second[0], dims, preferred_element_type=jnp.float32
        )
        rest[...] += cross * cross
    picked[0, :half] = rest[:, :half] + rest[:, half:]
    picked[1] = most[:, :half] + most[:, half:width]
    picked[2] = most[:, width : width + half] + most[:, width + half :]
    copies = []
    for p in range(power_ref.shape[0]):
        row = pl.multiple_of(slots_ref[p, 0] * half, half)
        power = picked[slots_ref[p, 1] - 1, pl.ds(row, half), :] / (bins * records)
        made[p] = jnp.where(p < count_ref[0], power, 0.0)
        copies.append(pltpu.make_async_copy(made.at[p], power_ref.at[p], sems.at[p]))
        copies[-1].start()
    for copy in copies:
        copy.wait()


def pair_powers(slots, count, held, bins):
    records, rows, width = held.shape
    half = width // 2
    return pl.pallas_call(
        functools.partial(pair_kernel, bins),
        out_shape=jax.ShapeDtypeStruct((slots.shape[0], half, half), jnp.float32),
        in_specs=[
            pl.BlockSpec(memory_space=pltpu.SMEM),
            pl.BlockSpec(memory_space=pltpu.SMEM),
            pl.BlockSpec(memory_space=pltpu.VMEM),
        ],
        out_specs=pl.BlockSpec(memory_space=pl.ANY),
        scratch_shapes=[
            pltpu.VMEM((4, bins, records, width), jnp.bfloat16),
            pltpu.VMEM((3 * half, 2 * width), jnp.float32),
            pltpu.VMEM((half, width), jnp.float32),
            pltpu.VMEM((3, 3 * half, half), jnp.float32),
            pltpu.VMEM((slots.shape[0], half, half), jnp.float32),
            pltpu.SemaphoreType.DMA((slots.shape[0],)),
        ],
        compiler_params=pltpu.CompilerParams(vmem_limit_bytes=32 * 1024 * 1024),
        cost_estimate=pl.CostEstimate(
            flops=2 * bins * 2 * records * 4 * half * 6 * half,
            bytes_accessed=held.size * 2,
            transcendentals=0,
        ),
    )(slots, count, held)


def exchange(blocks, groups):
    return lax.all_to_all(
        blocks, "sub", split_axis=0, concat_axis=0, tiled=True, axis_index_groups=groups
    )


def shards(spectra, bin_freqs, station_offsets, beam_grid, owner_subarrays, pair_slots, pair_count):
    spectra = spectra[0]
    bins = spectra.shape[1]
    records = lax.axis_size("sub")
    grid = np.arange(records).reshape(-1, COLUMNS)
    order = np.roll(grid, (-FIRST[0], -FIRST[1]), (0, 1)).reshape(-1)
    wide = [order.tolist()]
    near = order.reshape(-1, NEAR).tolist()
    parts = exchange(energy_parts(spectra, NEAR), near)
    group = jnp.sum(parts, axis=0)
    group, spectra, bin_freqs, station_offsets, beam_grid, owner_subarrays = lax.optimization_barrier(
        (group, spectra, bin_freqs, station_offsets, beam_grid, owner_subarrays)
    )
    code = encode(group)
    code = exchange(jnp.broadcast_to(code[None], (records, *code.shape)), wide)
    matrix = steering(bin_freqs, station_offsets, beam_grid)
    owners = owner_subarrays.reshape(-1, COLUMNS, owner_subarrays.shape[1])
    owners = jnp.roll(owners, (-FIRST[0], -FIRST[1]), (0, 1)).reshape(owner_subarrays.shape)
    outgoing = outgoing_beams(owners, code, jnp.swapaxes(spectra, 0, 1), matrix, records * bins)
    held = exchange(outgoing, wide)
    return pair_powers(pair_slots[0], pair_count, held, bins)


def solution(mesh):
    return jax.shard_map(
        shards,
        mesh=mesh,
        in_specs=(
            P("sub", None, "band", None),
            P("band"),
            P(),
            P(),
            P(),
            P("sub", None, None),
            P("sub"),
        ),
        out_specs=P("sub", "band", None),
        check_vma=False,
    )
```

```python
import functools
import math

import jax
import jax.numpy as jnp
import numpy as np
from jax import lax
from jax.experimental import pallas as pl
from jax.experimental.pallas import tpu as pltpu
from jax.sharding import PartitionSpec as P

COLUMNS = 4
DEEP = 2
FIRST = (8, 2)

slow_step = 0.04
eps = 1e-06


def steering_kernel(freqs_ref, offsets_ref, grid_ref, matrix_ref, delay):
    stations, beams = delay.shape
    block = 32
    factor = stations ** (-0.5)
    quarter = (lax.broadcasted_iota(jnp.int32, (block, beams), 1) >= beams // 2).astype(jnp.int32)
    grid = jnp.concatenate([grid_ref[...], grid_ref[...]], axis=1)
    slow_x = ((grid & 15).astype(jnp.float32) - 7.5) * slow_step
    slow_y = ((grid >> 4).astype(jnp.float32) - 7.5) * slow_step
    east = jnp.swapaxes(jnp.broadcast_to(offsets_ref[0:1, :], (beams, stations)), 0, 1)
    north = jnp.swapaxes(jnp.broadcast_to(offsets_ref[1:2, :], (beams, stations)), 0, 1)
    delay[...] = slow_x * east + slow_y * north

    def one_bin(n, carry):
        for row in range(0, stations, block):
            phase = (2.0 * math.pi * freqs_ref[n]) * delay[row : row + block, :]
            turns = jnp.floor(phase * (2.0 / math.pi) + 0.5)
            rest = phase - turns * 1.5703125
            rest = rest - turns * 4.837512969970703125e-4
            rest = rest - turns * 7.54978995489188216e-8
            square = rest * rest
            sine = (-1.9515295891e-4 * square + 8.3321608736e-3) * square - 1.6666654611e-1
            sine = sine * square * rest + rest
            cosine = (2.443315711809948e-5 * square - 1.388731625493765e-3) * square
            cosine = (cosine + 4.166664568298827e-2) * square * square - 0.5 * square + 1.0
            which = turns.astype(jnp.int32) + quarter
            odd = (which & 1) == 1
            upper = jnp.where(odd, sine, cosine) * jnp.where(((which + 1) & 2) == 0, factor, -factor)
            lower = jnp.where(odd, cosine, sine) * jnp.where((which & 2) == 0, factor, -factor)
            matrix_ref[n, row : row + block, :] = upper.astype(jnp.bfloat16)
            matrix_ref[n, stations + row : stations + row + block, :] = lower.astype(jnp.bfloat16)
        return carry

    lax.fori_loop(0, matrix_ref.shape[0], one_bin, 0)


def steering(bin_freqs, station_offsets, beam_grid):
    bins, stations, beams = bin_freqs.shape[0], station_offsets.shape[1], 2 * beam_grid.shape[0]
    smem = pl.BlockSpec(memory_space=pltpu.SMEM)
    vmem = pl.BlockSpec(memory_space=pltpu.VMEM)
    return pl.pallas_call(
        steering_kernel,
        out_shape=jax.ShapeDtypeStruct((bins, 2 * stations, beams), jnp.bfloat16),
        in_specs=[smem, vmem, vmem],
        out_specs=vmem,
        scratch_shapes=[pltpu.VMEM((stations, beams), jnp.float32)],
        compiler_params=pltpu.CompilerParams(vmem_limit_bytes=16 * 1024 * 1024),
        cost_estimate=pl.CostEstimate(
            flops=30 * bins * stations * beams,
            bytes_accessed=4 * bins * stations * beams,
            transcendentals=0,
        ),
    )(bin_freqs, station_offsets, beam_grid[None])


def energies(spectra):
    half = spectra.shape[2] // 2
    values = spectra.astype(jnp.float32)
    real, imag = values[:, :, :half], values[:, :, half:]
    return jnp.sum(real * real + imag * imag, axis=1)


def encode(energy):
    scaled = jnp.square(energy * (1.0 / 256.0))
    return jnp.square(scaled).astype(jnp.bfloat16)


def decode(code):
    return jnp.sqrt(jnp.sqrt(code.astype(jnp.float32))) * 256.0


def beam_kernel(count, order, ids_ref, code_ref, spectra_ref, matrix_ref, out_ref, made, turned, chunk, sems):
    bins, subarrays, width = spectra_ref.shape
    held = ids_ref.shape[0]
    steps, per_step = chunk.shape[0], chunk.shape[1]
    groups = decode(code_ref[...]).reshape(-1, subarrays, width // 2)
    scale = lax.rsqrt(jnp.sum(groups, axis=0) / count + eps)
    scale = jnp.concatenate([scale, scale], axis=1)
    for n in range(bins):
        white = (spectra_ref[n].astype(jnp.float32) * scale).astype(jnp.bfloat16)
        made[n] = jnp.dot(
            white, matrix_ref[n], preferred_element_type=jnp.float32
        ).astype(jnp.bfloat16)
    turned[...] = jnp.swapaxes(made[...], 0, 1)
    copies = []
    for step in range(steps):
        for own in range(per_step):
            for h in range(held):
                chunk[step, own, h * bins : (h + 1) * bins] = turned[
                    ids_ref[h, order[step * per_step + own]]
                ]
        copies.append(
            pltpu.make_async_copy(
                chunk.at[step], out_ref.at[pl.ds(step * per_step, per_step)], sems.at[step]
            )
        )
        copies[-1].start()
    for copy in copies:
        copy.wait()


def outgoing_beams(ids, order, code, spectra, matrix, count):
    bins, subarrays, width = spectra.shape
    held, owners = ids.shape
    beams = matrix.shape[2]
    steps = 8
    smem = pl.BlockSpec(memory_space=pltpu.SMEM)
    vmem = pl.BlockSpec(memory_space=pltpu.VMEM)
    return pl.pallas_call(
        functools.partial(beam_kernel, count, order),
        out_shape=jax.ShapeDtypeStruct((owners, held * bins, beams), jnp.bfloat16),
        in_specs=[smem, vmem, vmem, vmem],
        out_specs=pl.BlockSpec(memory_space=pl.ANY),
        scratch_shapes=[
            pltpu.VMEM((bins, subarrays, beams), jnp.bfloat16),
            pltpu.VMEM((subarrays, bins, beams), jnp.bfloat16),
            pltpu.VMEM((steps, owners // steps, held * bins, beams), jnp.bfloat16),
            pltpu.SemaphoreType.DMA((steps,)),
        ],
        compiler_params=pltpu.CompilerParams(vmem_limit_bytes=32 * 1024 * 1024),
        cost_estimate=pl.CostEstimate(
            flops=2 * bins * subarrays * width * beams,
            bytes_accessed=2 * (spectra.size + owners * held * bins * beams),
            transcendentals=0,
        ),
    )(ids, code, spectra, matrix)


def pair_kernel(bins, slots_ref, count_ref, held_ref, power_ref, turned_ref, most, rest, picked, made, sems):
    records, _, width = held_ref.shape
    half = width // 2
    for h in range(4):
        turned_ref[h] = jnp.swapaxes(held_ref[:, h * bins : (h + 1) * bins, :], 0, 1)
    low = lax.broadcasted_iota(jnp.int32, (records, width), 1) < half
    most[...] = jnp.zeros_like(most)
    rest[...] = jnp.zeros_like(rest)
    for n in range(bins):
        held = [turned_ref[h, n] for h in range(4)]
        rolled = [pltpu.roll(x, half, 1) for x in held]
        real = jnp.concatenate([jnp.where(low, held[0], rolled[1]), held[2]], axis=1)
        imag = jnp.concatenate([jnp.where(low, rolled[0], held[1]), rolled[2]], axis=1)
        first = jnp.concatenate([real, imag], axis=0)[:, : 3 * half]
        second = [
            jnp.concatenate([jnp.where(low, held[h], -held[h]), rolled[h]], axis=0)
            for h in range(1, 4)
        ]
        two = jnp.concatenate(second[1:], axis=1)
        dims = (((0,), (0,)), ((), ()))
        cross = lax.dot_general(first, two, dims, preferred_element_type=jnp.float32)
        most[...] += cross * cross
        cross = lax.dot_general(
            first[:, :half], second[0], dims, preferred_element_type=jnp.float32
        )
        rest[...] += cross * cross
    picked[0, :half] = rest[:, :half] + rest[:, half:]
    picked[1] = most[:, :half] + most[:, half:width]
    picked[2] = most[:, width : width + half] + most[:, width + half :]
    copies = []
    for p in range(power_ref.shape[0]):
        row = pl.multiple_of(slots_ref[0, p] * half, half)
        power = picked[slots_ref[1, p] - 1, pl.ds(row, half), :] / (bins * records)
        made[p] = jnp.where(p < count_ref[0], power, 0.0)
        copies.append(pltpu.make_async_copy(made.at[p], power_ref.at[p], sems.at[p]))
        copies[-1].start()
    for copy in copies:
        copy.wait()


def pair_powers(slots, count, held, bins):
    records, rows, width = held.shape
    half = width // 2
    return pl.pallas_call(
        functools.partial(pair_kernel, bins),
        out_shape=jax.ShapeDtypeStruct((slots.shape[1], half, half), jnp.float32),
        in_specs=[
            pl.BlockSpec(memory_space=pltpu.SMEM),
            pl.BlockSpec(memory_space=pltpu.SMEM),
            pl.BlockSpec(memory_space=pltpu.VMEM),
        ],
        out_specs=pl.BlockSpec(memory_space=pl.ANY),
        scratch_shapes=[
            pltpu.VMEM((4, bins, records, width), jnp.bfloat16),
            pltpu.VMEM((3 * half, 2 * width), jnp.float32),
            pltpu.VMEM((half, width), jnp.float32),
            pltpu.VMEM((3, 3 * half, half), jnp.float32),
            pltpu.VMEM((slots.shape[1], half, half), jnp.float32),
            pltpu.SemaphoreType.DMA((slots.shape[1],)),
        ],
        compiler_params=pltpu.CompilerParams(vmem_limit_bytes=32 * 1024 * 1024),
        cost_estimate=pl.CostEstimate(
            flops=2 * bins * 2 * records * 4 * half * 6 * half,
            bytes_accessed=held.size * 2,
            transcendentals=0,
        ),
    )(slots, count, held)


def exchange(blocks, groups):
    return lax.all_to_all(
        blocks, "sub", split_axis=0, concat_axis=0, tiled=True, axis_index_groups=groups
    )


def shards(spectra, bin_freqs, station_offsets, beam_grid, owner_subarrays, pair_slots, pair_count):
    spectra = spectra[0]
    bins = spectra.shape[1]
    records = lax.axis_size("sub")
    grid = np.arange(records).reshape(-1, COLUMNS)
    order = np.roll(grid, (-FIRST[0], -FIRST[1]), (0, 1))
    wide = [order.reshape(-1).tolist()]
    near = order.reshape(-1, DEEP * COLUMNS).tolist()
    along = order.T.tolist()
    energy = energies(spectra)
    parts = energy.reshape(DEEP, 1, -1, energy.shape[1])
    parts = jnp.broadcast_to(parts, (DEEP, COLUMNS, *parts.shape[2:]))
    parts = exchange(parts.reshape(-1, *parts.shape[2:]), near)
    code = encode(jnp.sum(parts, axis=0))
    code = jnp.broadcast_to(code[None], (order.shape[0], *code.shape))
    code, bin_freqs, station_offsets, beam_grid, owner_subarrays = lax.optimization_barrier(
        (code, bin_freqs, station_offsets, beam_grid, owner_subarrays)
    )
    code = exchange(code, along)
    matrix = steering(bin_freqs, station_offsets, beam_grid)
    spectra = jnp.swapaxes(spectra, 0, 1)
    outgoing = outgoing_beams(owner_subarrays.T, wide[0], code, spectra, matrix, records * bins)
    held = exchange(outgoing, wide)
    return pair_powers(pair_slots[0].T, pair_count, held, bins)


def solution(mesh):
    return jax.shard_map(
        shards,
        mesh=mesh,
        in_specs=(
            P("sub", None, "band", None),
            P("band"),
            P(),
            P(),
            P(),
            P("sub", None, None),
            P("sub"),
        ),
        out_specs=P("sub", "band", None),
        check_vma=False,
    )
```

```python
import functools
import math

import jax
import jax.numpy as jnp
import numpy as np
from jax import lax
from jax.experimental import pallas as pl
from jax.experimental.pallas import tpu as pltpu
from jax.sharding import PartitionSpec as P

COLUMNS = 4
DEEP = 2
FIRST = (8, 2)
ALONG = 10

slow_step = 0.04
eps = 1e-06


def steering_kernel(freqs_ref, offsets_ref, grid_ref, matrix_ref, delay):
    stations, beams = delay.shape
    block = 32
    factor = stations ** (-0.5)
    quarter = (lax.broadcasted_iota(jnp.int32, (block, beams), 1) >= beams // 2).astype(jnp.int32)
    grid = jnp.concatenate([grid_ref[...], grid_ref[...]], axis=1)
    slow_x = ((grid & 15).astype(jnp.float32) - 7.5) * slow_step
    slow_y = ((grid >> 4).astype(jnp.float32) - 7.5) * slow_step
    east = jnp.swapaxes(jnp.broadcast_to(offsets_ref[0:1, :], (beams, stations)), 0, 1)
    north = jnp.swapaxes(jnp.broadcast_to(offsets_ref[1:2, :], (beams, stations)), 0, 1)
    delay[...] = slow_x * east + slow_y * north

    def one_bin(n, carry):
        for row in range(0, stations, block):
            phase = (2.0 * math.pi * freqs_ref[n]) * delay[row : row + block, :]
            turns = jnp.floor(phase * (2.0 / math.pi) + 0.5)
            rest = phase - turns * 1.5703125
            rest = rest - turns * 4.837512969970703125e-4
            rest = rest - turns * 7.54978995489188216e-8
            square = rest * rest
            sine = (-1.9515295891e-4 * square + 8.3321608736e-3) * square - 1.6666654611e-1
            sine = sine * square * rest + rest
            cosine = (2.443315711809948e-5 * square - 1.388731625493765e-3) * square
            cosine = (cosine + 4.166664568298827e-2) * square * square - 0.5 * square + 1.0
            which = turns.astype(jnp.int32) + quarter
            odd = (which & 1) == 1
            upper = jnp.where(odd, sine, cosine) * jnp.where(((which + 1) & 2) == 0, factor, -factor)
            lower = jnp.where(odd, cosine, sine) * jnp.where((which & 2) == 0, factor, -factor)
            matrix_ref[n, row : row + block, :] = upper.astype(jnp.bfloat16)
            matrix_ref[n, stations + row : stations + row + block, :] = lower.astype(jnp.bfloat16)
        return carry

    lax.fori_loop(0, matrix_ref.shape[0], one_bin, 0)


def steering(bin_freqs, station_offsets, beam_grid):
    bins, stations, beams = bin_freqs.shape[0], station_offsets.shape[1], 2 * beam_grid.shape[0]
    smem = pl.BlockSpec(memory_space=pltpu.SMEM)
    vmem = pl.BlockSpec(memory_space=pltpu.VMEM)
    return pl.pallas_call(
        steering_kernel,
        out_shape=jax.ShapeDtypeStruct((bins, 2 * stations, beams), jnp.bfloat16),
        in_specs=[smem, vmem, vmem],
        out_specs=vmem,
        scratch_shapes=[pltpu.VMEM((stations, beams), jnp.float32)],
        compiler_params=pltpu.CompilerParams(vmem_limit_bytes=16 * 1024 * 1024),
        cost_estimate=pl.CostEstimate(
            flops=30 * bins * stations * beams,
            bytes_accessed=4 * bins * stations * beams,
            transcendentals=0,
        ),
    )(bin_freqs, station_offsets, beam_grid[None])


def energies(spectra):
    half = spectra.shape[2] // 2
    values = spectra.astype(jnp.float32)
    real, imag = values[:, :, :half], values[:, :, half:]
    return jnp.sum(real * real + imag * imag, axis=1)


def encode(energy):
    scaled = jnp.square(energy * (1.0 / 256.0))
    return jnp.square(scaled).astype(jnp.bfloat16)


def decode(code):
    return jnp.sqrt(jnp.sqrt(code.astype(jnp.float32))) * 256.0


def beam_kernel(
    count, order, ids_any, code_ref, spectra_ref, matrix_ref, out_ref, ids_ref, made, turned, chunk, sems, ids_sem
):
    ids_copy = pltpu.make_async_copy(ids_any, ids_ref, ids_sem)
    ids_copy.start()
    bins, subarrays, width = spectra_ref.shape
    held = ids_ref.shape[0]
    steps, per_step = chunk.shape[0], chunk.shape[1]
    groups = decode(code_ref[...]).reshape(-1, subarrays, width // 2)
    scale = lax.rsqrt(jnp.sum(groups, axis=0) / count + eps)
    scale = jnp.concatenate([scale, scale], axis=1)
    for n in range(bins):
        white = (spectra_ref[n].astype(jnp.float32) * scale).astype(jnp.bfloat16)
        made[n] = jnp.dot(
            white, matrix_ref[n], preferred_element_type=jnp.float32
        ).astype(jnp.bfloat16)
    turned[...] = jnp.swapaxes(made[...], 0, 1)
    ids_copy.wait()
    copies = []
    for step in range(steps):
        for own in range(per_step):
            for h in range(held):
                chunk[step, own, h * bins : (h + 1) * bins] = turned[
                    ids_ref[h, order[step * per_step + own]]
                ]
        copies.append(
            pltpu.make_async_copy(
                chunk.at[step], out_ref.at[pl.ds(step * per_step, per_step)], sems.at[step]
            )
        )
        copies[-1].start()
    for copy in copies:
        copy.wait()


def outgoing_beams(ids, order, code, spectra, matrix, count):
    bins, subarrays, width = spectra.shape
    held, owners = ids.shape
    beams = matrix.shape[2]
    steps = 8
    anywhere = pl.BlockSpec(memory_space=pl.ANY)
    vmem = pl.BlockSpec(memory_space=pltpu.VMEM)
    return pl.pallas_call(
        functools.partial(beam_kernel, count, order),
        out_shape=jax.ShapeDtypeStruct((owners, held * bins, beams), jnp.bfloat16),
        in_specs=[anywhere, vmem, vmem, vmem],
        out_specs=anywhere,
        scratch_shapes=[
            pltpu.SMEM(ids.shape, jnp.int32),
            pltpu.VMEM((bins, subarrays, beams), jnp.bfloat16),
            pltpu.VMEM((subarrays, bins, beams), jnp.bfloat16),
            pltpu.VMEM((steps, owners // steps, held * bins, beams), jnp.bfloat16),
            pltpu.SemaphoreType.DMA((steps,)),
            pltpu.SemaphoreType.DMA,
        ],
        compiler_params=pltpu.CompilerParams(vmem_limit_bytes=32 * 1024 * 1024),
        cost_estimate=pl.CostEstimate(
            flops=2 * bins * subarrays * width * beams,
            bytes_accessed=2 * (spectra.size + owners * held * bins * beams),
            transcendentals=0,
        ),
    )(ids, code, spectra, matrix)


def pair_kernel(
    bins, slots_any, count_any, held_ref, power_ref, slots_ref, count_ref, most, rest, picked, made, sems, slot_sems
):
    slot_copies = [
        pltpu.make_async_copy(slots_any, slots_ref, slot_sems.at[0]),
        pltpu.make_async_copy(count_any, count_ref, slot_sems.at[1]),
    ]
    for copy in slot_copies:
        copy.start()
    records, _, width = held_ref.shape
    half = width // 2
    turned = [
        jnp.swapaxes(held_ref[:, h * bins : (h + 1) * bins, :], 0, 1) for h in range(4)
    ]
    low = lax.broadcasted_iota(jnp.int32, (records, width), 1) < half
    for n in range(bins):
        held = [turned[h][n] for h in range(4)]
        rolled = [pltpu.roll(x, half, 1) for x in held]
        real = jnp.concatenate([jnp.where(low, held[0], rolled[1]), held[2]], axis=1)
        imag = jnp.concatenate([jnp.where(low, rolled[0], held[1]), rolled[2]], axis=1)
        first = jnp.concatenate([real, imag], axis=0)[:, : 3 * half]
        second = [
            jnp.concatenate([jnp.where(low, held[h], -held[h]), rolled[h]], axis=0)
            for h in range(1, 4)
        ]
        two = jnp.concatenate(second[1:], axis=1)
        dims = (((0,), (0,)), ((), ()))
        cross = lax.dot_general(first, two, dims, preferred_element_type=jnp.float32)
        most[...] = cross * cross if n == 0 else most[...] + cross * cross
        cross = lax.dot_general(
            first[:, :half], second[0], dims, preferred_element_type=jnp.float32
        )
        rest[...] = cross * cross if n == 0 else rest[...] + cross * cross
    picked[0, :half] = rest[:, :half] + rest[:, half:]
    picked[1] = most[:, :half] + most[:, half:width]
    picked[2] = most[:, width : width + half] + most[:, width + half :]
    for copy in slot_copies:
        copy.wait()
    copies = []
    for p in range(power_ref.shape[0]):
        row = pl.multiple_of(slots_ref[0, p] * half, half)
        power = picked[slots_ref[1, p] - 1, pl.ds(row, half), :] / (bins * records)
        made[p] = jnp.where(p < count_ref[0], power, 0.0)
        copies.append(pltpu.make_async_copy(made.at[p], power_ref.at[p], sems.at[p]))
        copies[-1].start()
    for copy in copies:
        copy.wait()


def pair_powers(slots, count, held, bins):
    records, rows, width = held.shape
    half = width // 2
    return pl.pallas_call(
        functools.partial(pair_kernel, bins),
        out_shape=jax.ShapeDtypeStruct((slots.shape[1], half, half), jnp.float32),
        in_specs=[
            pl.BlockSpec(memory_space=pl.ANY),
            pl.BlockSpec(memory_space=pl.ANY),
            pl.BlockSpec(memory_space=pltpu.VMEM),
        ],
        out_specs=pl.BlockSpec(memory_space=pl.ANY),
        scratch_shapes=[
            pltpu.SMEM(slots.shape, jnp.int32),
            pltpu.SMEM(count.shape, jnp.int32),
            pltpu.VMEM((3 * half, 2 * width), jnp.float32),
            pltpu.VMEM((half, width), jnp.float32),
            pltpu.VMEM((3, 3 * half, half), jnp.float32),
            pltpu.VMEM((slots.shape[1], half, half), jnp.float32),
            pltpu.SemaphoreType.DMA((slots.shape[1],)),
            pltpu.SemaphoreType.DMA((2,)),
        ],
        compiler_params=pltpu.CompilerParams(vmem_limit_bytes=32 * 1024 * 1024),
        cost_estimate=pl.CostEstimate(
            flops=2 * bins * 2 * records * 4 * half * 6 * half,
            bytes_accessed=held.size * 2,
            transcendentals=0,
        ),
    )(slots, count, held)


def exchange(blocks, groups):
    return lax.all_to_all(
        blocks, "sub", split_axis=0, concat_axis=0, tiled=True, axis_index_groups=groups
    )


def shards(spectra, bin_freqs, station_offsets, beam_grid, owner_subarrays, pair_slots, pair_count):
    spectra = spectra[0]
    bins = spectra.shape[1]
    records = lax.axis_size("sub")
    grid = np.arange(records).reshape(-1, COLUMNS)
    order = np.roll(grid, (-FIRST[0], -FIRST[1]), (0, 1))
    wide = [order.reshape(-1).tolist()]
    near = order.reshape(-1, DEEP * COLUMNS).tolist()
    along = np.roll(grid, -ALONG, 0).T.tolist()
    energy = energies(spectra)
    parts = energy.reshape(DEEP, 1, -1, energy.shape[1])
    parts = jnp.broadcast_to(parts, (DEEP, COLUMNS, *parts.shape[2:]))
    parts = exchange(parts.reshape(-1, *parts.shape[2:]), near)
    code = encode(jnp.sum(parts, axis=0))
    code = jnp.broadcast_to(code[None], (order.shape[0], *code.shape))
    code, bin_freqs, station_offsets, beam_grid, owner_subarrays = lax.optimization_barrier(
        (code, bin_freqs, station_offsets, beam_grid, owner_subarrays)
    )
    code = exchange(code, along)
    matrix = steering(bin_freqs, station_offsets, beam_grid)
    spectra = jnp.swapaxes(spectra, 0, 1)
    outgoing = outgoing_beams(owner_subarrays.T, wide[0], code, spectra, matrix, records * bins)
    held = exchange(outgoing, wide)
    return pair_powers(pair_slots[0].T, pair_count, held, bins)


def solution(mesh):
    return jax.shard_map(
        shards,
        mesh=mesh,
        in_specs=(
            P("sub", None, "band", None),
            P("band"),
            P(),
            P(),
            P(),
            P("sub", None, None),
            P("sub"),
        ),
        out_specs=P("sub", "band", None),
        check_vma=False,
    )
```

```python
import functools
import math

import jax
import jax.numpy as jnp
import numpy as np
from jax import lax
from jax.experimental import pallas as pl
from jax.experimental.pallas import tpu as pltpu
from jax.sharding import PartitionSpec as P

COLUMNS = 4
DEEP = 2
FIRST = (8, 2)
ALONG = 10

slow_step = 0.04
eps = 1e-06


def steering_kernel(freqs_ref, offsets_ref, grid_ref, matrix_ref, delay):
    stations, beams = delay.shape
    block = 32
    factor = stations ** (-0.5)
    quarter = (lax.broadcasted_iota(jnp.int32, (block, beams), 1) >= beams // 2).astype(jnp.int32)
    grid = jnp.concatenate([grid_ref[...], grid_ref[...]], axis=1)
    slow_x = ((grid & 15).astype(jnp.float32) - 7.5) * slow_step
    slow_y = ((grid >> 4).astype(jnp.float32) - 7.5) * slow_step
    east = jnp.swapaxes(jnp.broadcast_to(offsets_ref[0:1, :], (beams, stations)), 0, 1)
    north = jnp.swapaxes(jnp.broadcast_to(offsets_ref[1:2, :], (beams, stations)), 0, 1)
    delay[...] = slow_x * east + slow_y * north

    def one_bin(n, carry):
        for row in range(0, stations, block):
            phase = (2.0 * math.pi * freqs_ref[n]) * delay[row : row + block, :]
            turns = jnp.floor(phase * (2.0 / math.pi) + 0.5)
            rest = phase - turns * 1.5703125
            rest = rest - turns * 4.837512969970703125e-4
            rest = rest - turns * 7.54978995489188216e-8
            square = rest * rest
            sine = (-1.9515295891e-4 * square + 8.3321608736e-3) * square - 1.6666654611e-1
            sine = sine * square * rest + rest
            cosine = (2.443315711809948e-5 * square - 1.388731625493765e-3) * square
            cosine = (cosine + 4.166664568298827e-2) * square * square - 0.5 * square + 1.0
            which = turns.astype(jnp.int32) + quarter
            odd = (which & 1) == 1
            upper = jnp.where(odd, sine, cosine) * jnp.where(((which + 1) & 2) == 0, factor, -factor)
            lower = jnp.where(odd, cosine, sine) * jnp.where((which & 2) == 0, factor, -factor)
            matrix_ref[n, row : row + block, :] = upper.astype(jnp.bfloat16)
            matrix_ref[n, stations + row : stations + row + block, :] = lower.astype(jnp.bfloat16)
        return carry

    lax.fori_loop(0, matrix_ref.shape[0], one_bin, 0)


def steering(bin_freqs, station_offsets, beam_grid):
    bins, stations, beams = bin_freqs.shape[0], station_offsets.shape[1], 2 * beam_grid.shape[0]
    smem = pl.BlockSpec(memory_space=pltpu.SMEM)
    vmem = pl.BlockSpec(memory_space=pltpu.VMEM)
    return pl.pallas_call(
        steering_kernel,
        out_shape=jax.ShapeDtypeStruct((bins, 2 * stations, beams), jnp.bfloat16),
        in_specs=[smem, vmem, vmem],
        out_specs=vmem,
        scratch_shapes=[pltpu.VMEM((stations, beams), jnp.float32)],
        compiler_params=pltpu.CompilerParams(vmem_limit_bytes=16 * 1024 * 1024),
        cost_estimate=pl.CostEstimate(
            flops=30 * bins * stations * beams,
            bytes_accessed=4 * bins * stations * beams,
            transcendentals=0,
        ),
    )(bin_freqs, station_offsets, beam_grid[None])


def energies(spectra):
    half = spectra.shape[2] // 2
    values = spectra.astype(jnp.float32)
    real, imag = values[:, :, :half], values[:, :, half:]
    return jnp.sum(real * real + imag * imag, axis=1)


def encode(energy):
    scaled = jnp.square(energy * (1.0 / 256.0))
    return jnp.square(scaled).astype(jnp.bfloat16)


def decode(code):
    return jnp.sqrt(jnp.sqrt(code.astype(jnp.float32))) * 256.0


def beam_kernel(
    count, order, ids_any, code_ref, spectra_ref, matrix_ref, out_ref, ids_ref, made, turned, chunk, sems, ids_sem
):
    ids_copy = pltpu.make_async_copy(ids_any, ids_ref, ids_sem)
    ids_copy.start()
    bins, subarrays, width = spectra_ref.shape
    held = ids_ref.shape[0]
    steps, per_step = chunk.shape[0], chunk.shape[1]
    groups = decode(code_ref[...]).reshape(-1, subarrays, width // 2)
    scale = lax.rsqrt(jnp.sum(groups, axis=0) / count + eps)
    scale = jnp.concatenate([scale, scale], axis=1)
    for n in range(bins):
        white = (spectra_ref[n].astype(jnp.float32) * scale).astype(jnp.bfloat16)
        made[n] = jnp.dot(
            white, matrix_ref[n], preferred_element_type=jnp.float32
        ).astype(jnp.bfloat16)
    turned[...] = jnp.swapaxes(made[...], 0, 1)
    ids_copy.wait()
    copies = []
    for step in range(steps):
        for own in range(per_step):
            for h in range(held):
                chunk[step, own, h * bins : (h + 1) * bins] = turned[
                    ids_ref[h, order[step * per_step + own]]
                ]
        copies.append(
            pltpu.make_async_copy(
                chunk.at[step], out_ref.at[pl.ds(step * per_step, per_step)], sems.at[step]
            )
        )
        copies[-1].start()
    for copy in copies:
        copy.wait()


def outgoing_beams(ids, order, code, spectra, matrix, count):
    bins, subarrays, width = spectra.shape
    held, owners = ids.shape
    beams = matrix.shape[2]
    steps = 8
    anywhere = pl.BlockSpec(memory_space=pl.ANY)
    vmem = pl.BlockSpec(memory_space=pltpu.VMEM)
    return pl.pallas_call(
        functools.partial(beam_kernel, count, order),
        out_shape=jax.ShapeDtypeStruct((owners, held * bins, beams), jnp.bfloat16),
        in_specs=[anywhere, vmem, vmem, vmem],
        out_specs=anywhere,
        scratch_shapes=[
            pltpu.SMEM(ids.shape, jnp.int32),
            pltpu.VMEM((bins, subarrays, beams), jnp.bfloat16),
            pltpu.VMEM((subarrays, bins, beams), jnp.bfloat16),
            pltpu.VMEM((steps, owners // steps, held * bins, beams), jnp.bfloat16),
            pltpu.SemaphoreType.DMA((steps,)),
            pltpu.SemaphoreType.DMA,
        ],
        compiler_params=pltpu.CompilerParams(vmem_limit_bytes=32 * 1024 * 1024),
        cost_estimate=pl.CostEstimate(
            flops=2 * bins * subarrays * width * beams,
            bytes_accessed=2 * (spectra.size + owners * held * bins * beams),
            transcendentals=0,
        ),
    )(ids, code, spectra, matrix)


def pair_kernel(
    bins, slots_any, count_any, held_ref, power_ref, slots_ref, count_ref, most, rest, picked, slot_sems
):
    slot_copies = [
        pltpu.make_async_copy(slots_any, slots_ref, slot_sems.at[0]),
        pltpu.make_async_copy(count_any, count_ref, slot_sems.at[1]),
    ]
    for copy in slot_copies:
        copy.start()
    records, _, width = held_ref.shape
    half = width // 2
    turned = [
        jnp.swapaxes(held_ref[:, h * bins : (h + 1) * bins, :], 0, 1) for h in range(4)
    ]
    low = lax.broadcasted_iota(jnp.int32, (records, width), 1) < half
    for n in range(bins):
        held = [turned[h][n] for h in range(4)]
        rolled = [pltpu.roll(x, half, 1) for x in held]
        real = jnp.concatenate([jnp.where(low, held[0], rolled[1]), held[2]], axis=1)
        imag = jnp.concatenate([jnp.where(low, rolled[0], held[1]), rolled[2]], axis=1)
        first = jnp.concatenate([real, imag], axis=0)[:, : 3 * half]
        second = [
            jnp.concatenate([jnp.where(low, held[h], -held[h]), rolled[h]], axis=0)
            for h in range(1, 4)
        ]
        two = jnp.concatenate(second[1:], axis=1)
        dims = (((0,), (0,)), ((), ()))
        cross = lax.dot_general(first, two, dims, preferred_element_type=jnp.float32)
        most[...] = cross * cross if n == 0 else most[...] + cross * cross
        cross = lax.dot_general(
            first[:, :half], second[0], dims, preferred_element_type=jnp.float32
        )
        rest[...] = cross * cross if n == 0 else rest[...] + cross * cross
    picked[0, :half] = rest[:, :half] + rest[:, half:]
    picked[1] = most[:, :half] + most[:, half:width]
    picked[2] = most[:, width : width + half] + most[:, width + half :]
    for copy in slot_copies:
        copy.wait()
    for p in range(power_ref.shape[0]):
        row = pl.multiple_of(slots_ref[0, p] * half, half)
        power = picked[slots_ref[1, p] - 1, pl.ds(row, half), :] / (bins * records)
        power_ref[p] = jnp.where(p < count_ref[0], power, 0.0)


def pair_powers(slots, count, held, bins):
    records, rows, width = held.shape
    half = width // 2
    return pl.pallas_call(
        functools.partial(pair_kernel, bins),
        out_shape=jax.ShapeDtypeStruct((slots.shape[1], half, half), jnp.float32),
        in_specs=[
            pl.BlockSpec(memory_space=pl.ANY),
            pl.BlockSpec(memory_space=pl.ANY),
            pl.BlockSpec(memory_space=pltpu.VMEM),
        ],
        out_specs=pl.BlockSpec(memory_space=pltpu.VMEM),
        scratch_shapes=[
            pltpu.SMEM(slots.shape, jnp.int32),
            pltpu.SMEM(count.shape, jnp.int32),
            pltpu.VMEM((3 * half, 2 * width), jnp.float32),
            pltpu.VMEM((half, width), jnp.float32),
            pltpu.VMEM((3, 3 * half, half), jnp.float32),
            pltpu.SemaphoreType.DMA((2,)),
        ],
        compiler_params=pltpu.CompilerParams(vmem_limit_bytes=32 * 1024 * 1024),
        cost_estimate=pl.CostEstimate(
            flops=2 * bins * 2 * records * 4 * half * 6 * half,
            bytes_accessed=held.size * 2,
            transcendentals=0,
        ),
    )(slots, count, held)


def exchange(blocks, groups):
    return lax.all_to_all(
        blocks, "sub", split_axis=0, concat_axis=0, tiled=True, axis_index_groups=groups
    )


def shards(spectra, bin_freqs, station_offsets, beam_grid, owner_subarrays, pair_slots, pair_count):
    spectra = spectra[0]
    bins = spectra.shape[1]
    records = lax.axis_size("sub")
    grid = np.arange(records).reshape(-1, COLUMNS)
    order = np.roll(grid, (-FIRST[0], -FIRST[1]), (0, 1))
    wide = [order.reshape(-1).tolist()]
    near = np.roll(grid, -2, 1).reshape(-1, DEEP * COLUMNS).tolist()
    along = np.roll(grid, -ALONG, 0).T.tolist()
    energy = energies(spectra)
    parts = energy.reshape(DEEP, 1, -1, energy.shape[1])
    parts = jnp.broadcast_to(parts, (DEEP, COLUMNS, *parts.shape[2:]))
    parts = exchange(parts.reshape(-1, *parts.shape[2:]), near)
    code = encode(jnp.sum(parts, axis=0))
    code = jnp.broadcast_to(code[None], (order.shape[0], *code.shape))
    code, bin_freqs, station_offsets, beam_grid, owner_subarrays = lax.optimization_barrier(
        (code, bin_freqs, station_offsets, beam_grid, owner_subarrays)
    )
    code = exchange(code, along)
    matrix = steering(bin_freqs, station_offsets, beam_grid)
    spectra = jnp.swapaxes(spectra, 0, 1)
    outgoing = outgoing_beams(owner_subarrays.T, wide[0], code, spectra, matrix, records * bins)
    held = exchange(outgoing, wide)
    return pair_powers(pair_slots[0].T, pair_count, held, bins)


def solution(mesh):
    return jax.shard_map(
        shards,
        mesh=mesh,
        in_specs=(
            P("sub", None, "band", None),
            P("band"),
            P(),
            P(),
            P(),
            P("sub", None, None),
            P("sub"),
        ),
        out_specs=P("sub", "band", None),
        check_vma=False,
    )
```

```python
import functools
import math

import jax
import jax.numpy as jnp
import numpy as np
from jax import lax
from jax.experimental import pallas as pl
from jax.experimental.pallas import tpu as pltpu
from jax.sharding import PartitionSpec as P

COLUMNS = 4
DEEP = 2
FIRST = (8, 2)
ALONG = 10

slow_step = 0.04
eps = 1e-06


def steering_kernel(freqs_ref, offsets_ref, grid_ref, matrix_ref, delay):
    stations, beams = delay.shape
    block = 32
    factor = stations ** (-0.5)
    quarter = (lax.broadcasted_iota(jnp.int32, (block, beams), 1) >= beams // 2).astype(jnp.int32)
    grid = jnp.concatenate([grid_ref[...], grid_ref[...]], axis=1)
    slow_x = ((grid & 15).astype(jnp.float32) - 7.5) * slow_step
    slow_y = ((grid >> 4).astype(jnp.float32) - 7.5) * slow_step
    east = jnp.swapaxes(jnp.broadcast_to(offsets_ref[0:1, :], (beams, stations)), 0, 1)
    north = jnp.swapaxes(jnp.broadcast_to(offsets_ref[1:2, :], (beams, stations)), 0, 1)
    delay[...] = slow_x * east + slow_y * north

    def one_bin(n, carry):
        for row in range(0, stations, block):
            phase = (2.0 * math.pi * freqs_ref[n]) * delay[row : row + block, :]
            turns = jnp.floor(phase * (2.0 / math.pi) + 0.5)
            rest = phase - turns * 1.5703125
            rest = rest - turns * 4.837512969970703125e-4
            rest = rest - turns * 7.54978995489188216e-8
            square = rest * rest
            sine = (-1.9515295891e-4 * square + 8.3321608736e-3) * square - 1.6666654611e-1
            sine = sine * square * rest + rest
            cosine = (2.443315711809948e-5 * square - 1.388731625493765e-3) * square
            cosine = (cosine + 4.166664568298827e-2) * square * square - 0.5 * square + 1.0
            which = turns.astype(jnp.int32) + quarter
            odd = (which & 1) == 1
            upper = jnp.where(odd, sine, cosine) * jnp.where(((which + 1) & 2) == 0, factor, -factor)
            lower = jnp.where(odd, cosine, sine) * jnp.where((which & 2) == 0, factor, -factor)
            matrix_ref[n, row : row + block, :] = upper.astype(jnp.bfloat16)
            matrix_ref[n, stations + row : stations + row + block, :] = lower.astype(jnp.bfloat16)
        return carry

    lax.fori_loop(0, matrix_ref.shape[0], one_bin, 0)


def steering(bin_freqs, station_offsets, beam_grid):
    bins, stations, beams = bin_freqs.shape[0], station_offsets.shape[1], 2 * beam_grid.shape[0]
    smem = pl.BlockSpec(memory_space=pltpu.SMEM)
    vmem = pl.BlockSpec(memory_space=pltpu.VMEM)
    return pl.pallas_call(
        steering_kernel,
        out_shape=jax.ShapeDtypeStruct((bins, 2 * stations, beams), jnp.bfloat16),
        in_specs=[smem, vmem, vmem],
        out_specs=vmem,
        scratch_shapes=[pltpu.VMEM((stations, beams), jnp.float32)],
        compiler_params=pltpu.CompilerParams(vmem_limit_bytes=16 * 1024 * 1024),
        cost_estimate=pl.CostEstimate(
            flops=30 * bins * stations * beams,
            bytes_accessed=4 * bins * stations * beams,
            transcendentals=0,
        ),
    )(bin_freqs, station_offsets, beam_grid[None])


def energies(spectra):
    half = spectra.shape[2] // 2
    values = spectra.astype(jnp.float32)
    real, imag = values[:, :, :half], values[:, :, half:]
    return jnp.sum(real * real + imag * imag, axis=1)


def encode(energy):
    scaled = jnp.square(energy * (1.0 / 256.0))
    return jnp.square(scaled).astype(jnp.bfloat16)


def decode(code):
    return jnp.sqrt(jnp.sqrt(code.astype(jnp.float32))) * 256.0


def beam_kernel(
    count, order, ids_any, code_ref, spectra_ref, matrix_ref, out_ref, ids_ref, made, turned, chunk, sems, ids_sem
):
    ids_copy = pltpu.make_async_copy(ids_any, ids_ref, ids_sem)
    ids_copy.start()
    bins, subarrays, width = spectra_ref.shape
    held = ids_ref.shape[0]
    steps, per_step = chunk.shape[0], chunk.shape[1]
    groups = decode(code_ref[...]).reshape(-1, subarrays, width // 2)
    scale = lax.rsqrt(jnp.sum(groups, axis=0) * (1.0 / count) + eps)
    scale = jnp.concatenate([scale, scale], axis=1)
    for n in range(bins):
        white = (spectra_ref[n].astype(jnp.float32) * scale).astype(jnp.bfloat16)
        made[n] = jnp.dot(
            white, matrix_ref[n], preferred_element_type=jnp.float32
        ).astype(jnp.bfloat16)
    turned[...] = jnp.swapaxes(made[...], 0, 1)
    ids_copy.wait()
    copies = []
    for step in range(steps):
        for own in range(per_step):
            for h in range(held):
                chunk[step, own, h * bins : (h + 1) * bins] = turned[
                    ids_ref[h, order[step * per_step + own]]
                ]
        copies.append(
            pltpu.make_async_copy(
                chunk.at[step], out_ref.at[pl.ds(step * per_step, per_step)], sems.at[step]
            )
        )
        copies[-1].start()
    for copy in copies:
        copy.wait()


def outgoing_beams(ids, order, code, spectra, matrix, count):
    bins, subarrays, width = spectra.shape
    held, owners = ids.shape
    beams = matrix.shape[2]
    steps = 8
    anywhere = pl.BlockSpec(memory_space=pl.ANY)
    vmem = pl.BlockSpec(memory_space=pltpu.VMEM)
    return pl.pallas_call(
        functools.partial(beam_kernel, count, order),
        out_shape=jax.ShapeDtypeStruct((owners, held * bins, beams), jnp.bfloat16),
        in_specs=[anywhere, vmem, vmem, vmem],
        out_specs=anywhere,
        scratch_shapes=[
            pltpu.SMEM(ids.shape, jnp.int32),
            pltpu.VMEM((bins, subarrays, beams), jnp.bfloat16),
            pltpu.VMEM((subarrays, bins, beams), jnp.bfloat16),
            pltpu.VMEM((steps, owners // steps, held * bins, beams), jnp.bfloat16),
            pltpu.SemaphoreType.DMA((steps,)),
            pltpu.SemaphoreType.DMA,
        ],
        compiler_params=pltpu.CompilerParams(vmem_limit_bytes=32 * 1024 * 1024),
        cost_estimate=pl.CostEstimate(
            flops=2 * bins * subarrays * width * beams,
            bytes_accessed=2 * (spectra.size + owners * held * bins * beams),
            transcendentals=0,
        ),
    )(ids, code, spectra, matrix)


def pair_kernel(
    bins, slots_any, count_any, held_ref, power_ref, slots_ref, count_ref, most, rest, picked, slot_sems
):
    slot_copies = [
        pltpu.make_async_copy(slots_any, slots_ref, slot_sems.at[0]),
        pltpu.make_async_copy(count_any, count_ref, slot_sems.at[1]),
    ]
    for copy in slot_copies:
        copy.start()
    records, _, width = held_ref.shape
    half = width // 2
    turned = [
        jnp.swapaxes(held_ref[:, h * bins : (h + 1) * bins, :], 0, 1) for h in range(4)
    ]
    low = lax.broadcasted_iota(jnp.int32, (records, width), 1) < half
    for n in range(bins):
        held = [turned[h][n] for h in range(4)]
        rolled = [pltpu.roll(x, half, 1) for x in held]
        real = jnp.concatenate([jnp.where(low, held[0], rolled[1]), held[2]], axis=1)
        imag = jnp.concatenate([jnp.where(low, rolled[0], held[1]), rolled[2]], axis=1)
        first = jnp.concatenate([real, imag], axis=0)[:, : 3 * half]
        second = [
            jnp.concatenate([jnp.where(low, held[h], -held[h]), rolled[h]], axis=0)
            for h in range(1, 4)
        ]
        two = jnp.concatenate(second[1:], axis=1)
        dims = (((0,), (0,)), ((), ()))
        cross = lax.dot_general(first, two, dims, preferred_element_type=jnp.float32)
        most[...] = cross * cross if n == 0 else most[...] + cross * cross
        cross = lax.dot_general(
            first[:, :half], second[0], dims, preferred_element_type=jnp.float32
        )
        rest[...] = cross * cross if n == 0 else rest[...] + cross * cross
    picked[0, :half] = rest[:, :half] + rest[:, half:]
    picked[1] = most[:, :half] + most[:, half:width]
    picked[2] = most[:, width : width + half] + most[:, width + half :]
    for copy in slot_copies:
        copy.wait()
    for p in range(power_ref.shape[0]):
        row = pl.multiple_of(slots_ref[0, p] * half, half)
        power = picked[slots_ref[1, p] - 1, pl.ds(row, half), :] * (1.0 / (bins * records))
        power_ref[p] = jnp.where(p < count_ref[0], power, 0.0)


def pair_powers(slots, count, held, bins):
    records, rows, width = held.shape
    half = width // 2
    return pl.pallas_call(
        functools.partial(pair_kernel, bins),
        out_shape=jax.ShapeDtypeStruct((slots.shape[1], half, half), jnp.float32),
        in_specs=[
            pl.BlockSpec(memory_space=pl.ANY),
            pl.BlockSpec(memory_space=pl.ANY),
            pl.BlockSpec(memory_space=pltpu.VMEM),
        ],
        out_specs=pl.BlockSpec(memory_space=pltpu.VMEM),
        scratch_shapes=[
            pltpu.SMEM(slots.shape, jnp.int32),
            pltpu.SMEM(count.shape, jnp.int32),
            pltpu.VMEM((3 * half, 2 * width), jnp.float32),
            pltpu.VMEM((half, width), jnp.float32),
            pltpu.VMEM((3, 3 * half, half), jnp.float32),
            pltpu.SemaphoreType.DMA((2,)),
        ],
        compiler_params=pltpu.CompilerParams(vmem_limit_bytes=32 * 1024 * 1024),
        cost_estimate=pl.CostEstimate(
            flops=2 * bins * 2 * records * 4 * half * 6 * half,
            bytes_accessed=held.size * 2,
            transcendentals=0,
        ),
    )(slots, count, held)


def exchange(blocks, groups):
    return lax.all_to_all(
        blocks, "sub", split_axis=0, concat_axis=0, tiled=True, axis_index_groups=groups
    )


def shards(spectra, bin_freqs, station_offsets, beam_grid, owner_subarrays, pair_slots, pair_count):
    spectra = spectra[0]
    bins = spectra.shape[1]
    records = lax.axis_size("sub")
    grid = np.arange(records).reshape(-1, COLUMNS)
    order = np.roll(grid, (-FIRST[0], -FIRST[1]), (0, 1))
    wide = [order.reshape(-1).tolist()]
    near = np.roll(grid, -2, 1).reshape(-1, DEEP * COLUMNS).tolist()
    along = np.roll(grid, -ALONG, 0).T.tolist()
    energy = energies(spectra)
    parts = energy.reshape(DEEP, 1, -1, energy.shape[1])
    parts = jnp.broadcast_to(parts, (DEEP, COLUMNS, *parts.shape[2:]))
    parts = exchange(parts.reshape(-1, *parts.shape[2:]), near)
    code = encode(jnp.sum(parts, axis=0))
    code = jnp.broadcast_to(code[None], (order.shape[0], *code.shape))
    code, bin_freqs, station_offsets, beam_grid, owner_subarrays = lax.optimization_barrier(
        (code, bin_freqs, station_offsets, beam_grid, owner_subarrays)
    )
    code = exchange(code, along)
    matrix = steering(bin_freqs, station_offsets, beam_grid)
    spectra = jnp.swapaxes(spectra, 0, 1)
    outgoing = outgoing_beams(owner_subarrays.T, wide[0], code, spectra, matrix, records * bins)
    held = exchange(outgoing, wide)
    return pair_powers(pair_slots[0].T, pair_count, held, bins)


def solution(mesh):
    return jax.shard_map(
        shards,
        mesh=mesh,
        in_specs=(
            P("sub", None, "band", None),
            P("band"),
            P(),
            P(),
            P(),
            P("sub", None, None),
            P("sub"),
        ),
        out_specs=P("sub", "band", None),
        check_vma=False,
    )
```
